512 devices in a mesh: filt: 32 (over z_lo, x, core), dp: 16 (over z_hi, y).
Axes of the slice: x: 4, y: 4, z: 16 (z_hi: 4, z_lo: 4; z = z_hi * 4 + z_lo), core: 2. Of those that a mesh axis runs over, the one named last changes fastest.
Arguments:
- activations: bfloat16 [16, 128, 4, 32, 128], P('dp', 'filt'), may hold values from -6 to 6
- weight_one: bfloat16 [3, 3, 3, 128, 128], P(None, None, None, None, 'filt'), may hold values from -0.109375 to 0.109375
- weight_two: bfloat16 [3, 3, 3, 128, 128], P(None, None, None, None, 'filt'), may hold values from -0.109375 to 0.109375
- grad_out: bfloat16 [16, 128, 4, 32, 128], P('dp', 'filt'), may hold values from -0.011962891 to 0.011962891
Outputs:
- out_two: bfloat16 [16, 128, 4, 32, 128], P('dp', 'filt')
- grad_one: float32 [3, 3, 3, 128, 128], P(None, None, None, None, 'filt')
- grad_two: float32 [3, 3, 3, 128, 128], P(None, None, None, None, 'filt')
The draws below stay inside these ranges and needn't reach their ends.
All inputs are finite; a program needn't handle non-finite values.
Results may differ from the reference program's by a relative error of at most 0.035.
The reference program's roundings to bfloat16 on the way (of `hidden`, `error_two` and `error_one`) count: a program that leaves them out, or rounds other values in their place, can miss the bound.
Values may be sent and summed in bfloat16 or wider, within the bound.
No kernel may reach another device: no remote copies, remote signals or barrier semaphores. Data moves between devices by JAX's collectives and lax.ppermute only.
A program may use at most 64 MiB of HBM per device.

```python
import jax
import jax.numpy as jnp
from jax import lax

C = 128
DZ = 4
W = 128
NX = 32
SAMPLES = 16


def block_levels(key, extent, shards, low, high):
    level, own = 1.0, jax.random.fold_in(key, 6)
    for axis_at, blocks in shards:
        heights = jnp.exp(jax.random.uniform(jax.random.fold_in(own, axis_at), (blocks,), jnp.float32, low / len(shards), high / len(shards)))
        level = level * jnp.repeat(heights, extent[axis_at] // blocks).reshape([-1 if axis == axis_at else 1 for axis in range(len(extent))])
    return level


def centred(own_key, dims, deviation, most, pieces=(), dtype=jnp.bfloat16):
    gain = block_levels(own_key, dims, pieces, -0.22, 0.18) if pieces else 1.0
    drawn = jax.random.normal(own_key, dims, jnp.float32) * deviation * gain
    return jnp.minimum(jnp.maximum(drawn, -most), most).astype(dtype)


def setup_inputs(seed: int = 0) -> dict:
    streams_of = jax.random.split(jax.random.key(seed), 5)
    return {
        "activations": centred(streams_of[0], (SAMPLES, C, DZ, NX, W), 1.0, 6.0, ((0, 16), (1, 32))),
        "weight_one": centred(streams_of[1], (3, 3, 3, C, C), (27 * C) ** -0.5, 0.109375, ((4, 32),)),
        "weight_two": centred(streams_of[2], (3, 3, 3, C, C), (27 * C) ** -0.5, 0.109375, ((4, 32),)),
        "grad_out": centred(streams_of[3], (SAMPLES, C, DZ, NX, W), 0.002, 0.011962891, ((0, 16), (1, 32))),
    }


SLOPE = 0.3

def convolve(volume, weight):
    return lax.conv_general_dilated(volume.astype(jnp.float32), weight.astype(jnp.float32), (1, 1, 1), [(1, 1), (1, 1), (1, 1)], dimension_numbers=('NCDHW', 'DHWIO', 'NCDHW'), precision=lax.Precision.HIGHEST)

def leaky_relu(values):
    return jnp.where(values > 0, values, SLOPE * values)

def slope_of(values):
    return jnp.where(values > 0, jnp.float32(1.0), jnp.float32(SLOPE))

def weight_grad(volume, errors):
    start = jnp.zeros((3, 3, 3, volume.shape[1], errors.shape[1]), jnp.float32)
    source = volume.astype(jnp.float32)
    _, pullback = jax.vjp(lambda weight: convolve(source, weight), start)
    return pullback(errors.astype(jnp.float32))[0]

def reference(activations, weight_one, weight_two, grad_out):
    pre_one = convolve(activations, weight_one)
    hidden = leaky_relu(pre_one).astype(jnp.bfloat16)
    pre_two = convolve(hidden, weight_two)
    out_two = leaky_relu(pre_two).astype(jnp.bfloat16)
    error_two = (grad_out.astype(jnp.float32) * slope_of(pre_two)).astype(jnp.bfloat16)
    flipped = jnp.transpose(weight_two[::-1, ::-1, ::-1], (0, 1, 2, 4, 3))
    back_one = convolve(error_two, flipped)
    error_one = (back_one * slope_of(pre_one)).astype(jnp.bfloat16)
    grad_two = weight_grad(hidden, error_two)
    grad_one = weight_grad(activations, error_one)
    return (out_two, grad_one, grad_two)
```

```python
import jax
import jax.numpy as jnp
import numpy as np
from jax import lax
from jax.experimental import pallas as pl
from jax.experimental.pallas import tpu as pltpu
from jax.sharding import Mesh, PartitionSpec as P

SLOPE = 0.3
CHIPS = ("zl", "x")
FILT = ("zl", "x", "c")
DP = ("zh", "y")
F32 = jnp.float32
BF16 = jnp.bfloat16
ROWS, COTS, TAPS = 8, 4, 28


def low_half(shape):
    return lax.broadcasted_iota(jnp.int32, shape, len(shape) - 2) < 4


def swap_halves(tiles):
    return pltpu.roll(tiles, 4, tiles.ndim - 2)


def merge(mine, other, core):
    low = low_half(mine.shape)
    first = jnp.where(low, mine, swap_halves(other))
    second = jnp.where(low, swap_halves(mine), other)
    return [pltpu.roll(plane, 4 * core, plane.ndim - 2) for plane in (first, second)]


def shift_lanes(block, by):
    lane = lax.broadcasted_iota(jnp.int32, block.shape, 1)
    edge = 0 if by > 0 else 127
    return jnp.where(lane == edge, 0.0, pltpu.roll(block, by % 128, 1))


def conv_plane(weights, source, depth, rows, first_row):
    low, high = max(depth - 1, 0), min(depth + 1, 3)
    taps = slice((low - depth + 1) * 128, (high - depth + 2) * 128)
    total = None
    for b in range(3):
        lanes = slice((first_row + b) * 128, (first_row + b + rows) * 128)
        part = jnp.dot(
            weights[b, :, taps],
            source[low * 128 : (high + 1) * 128, lanes],
            preferred_element_type=F32,
        )
        total = part if total is None else total + part
    out = []
    for r in range(rows):
        block = total[:, r * 128 : (r + 1) * 128]
        out.append(
            block[128:256] + shift_lanes(block[:128], 1) + shift_lanes(block[256:], -1)
        )
    return out


def own_rows(block, core):
    tiles = pltpu.roll(block.reshape(4, 4, 8, 128), (8 - 4 * core) % 8, 2)
    pairs = []
    for x in range(4):
        for zl in (0, 2):
            one, two = tiles[zl, x], tiles[zl + 1, x]
            pairs.append(jnp.where(low_half(one.shape), one, swap_halves(two)))
    return jnp.concatenate(pairs, 0)


def put_errors(shifted, block, core, depth, row):
    own = own_rows(block, core)
    lanes = slice((depth * 2 + row) * 128, (depth * 2 + row + 1) * 128)
    shifted[0:64, lanes] = shift_lanes(own, -1).astype(BF16)
    shifted[64:128, lanes] = own.astype(BF16)
    shifted[128:192, lanes] = shift_lanes(own, 1).astype(BF16)


def tap_grad(shifted, source, first_row, total, out, which):
    for b in range(3):
        lanes = slice((first_row + b) * 128, (first_row + b + 2) * 128)
        total[...] = jnp.zeros_like(total)
        for depth in range(4):
            low, high = max(depth - 1, 0), min(depth + 1, 3)
            taps = slice((low - depth + 1) * 128, (high - depth + 2) * 128)
            total[:, taps] += lax.dot_general(
                shifted[:, depth * 256 : (depth + 1) * 256],
                source[low * 128 : (high + 1) * 128, lanes],
                (((1,), (1,)), ((), ())),
                preferred_element_type=F32,
            )
        for a in range(3):
            for e in range(3):
                tap = a * 9 + b * 3 + e
                for x in range(4):
                    out[x, tap // 7, which * 7 + tap % 7] = total[
                        e * 64 + x * 16 : e * 64 + (x + 1) * 16, a * 128 : (a + 1) * 128
                    ].astype(BF16)


def work(
    place, mine, other, out_tiles, grads,
    act, hid, err, cot, w_one, w_two, w_back, pre, shifted, total,
):
    core, chip = place[0], place[1]

    def planes(step, h):
        one = mine[:, step].astype(F32).reshape(16, 2, 8, 128)[:, h]
        two = other[:, step].astype(F32).reshape(16, 2, 8, 128)[:, h]
        return [plane.reshape(128, 128) for plane in merge(one, two, core)]

    for r in range(ROWS):
        for h in range(2):
            for p, plane in enumerate(planes(r, h)):
                z = 2 * h + p
                act[z * 128 : (z + 1) * 128, r * 128 : (r + 1) * 128] = plane.astype(BF16)
    for layer in range(2):
        for step in range(7):
            for h in range(2):
                for p, plane in enumerate(planes(ROWS + COTS + layer * 7 + step, h)):
                    tap = 4 * step + 2 * h + p
                    if tap >= 27:
                        continue
                    a, b, e = tap // 9, tap // 3 % 3, tap % 3
                    into = w_two if layer else w_one
                    into[b, e * 128 : (e + 1) * 128, a * 128 : (a + 1) * 128] = plane.astype(BF16)
                    if layer:
                        a, b, e = 2 - a, 2 - b, 2 - e
                        w_back[b, e * 128 : (e + 1) * 128, a * 128 : (a + 1) * 128] = plane.T.astype(BF16)
    for r in range(COTS):
        for h in range(2):
            for p, plane in enumerate(planes(ROWS + r, h)):
                z = 2 * h + p
                cot[z * 128 : (z + 1) * 128, r * 128 : (r + 1) * 128] = plane

    for z in range(4):
        for r, value in enumerate(conv_plane(w_one, act, z, 6, 0)):
            row = 2 * chip - 2 + r
            inside = jnp.logical_and(row >= 0, row < 32)
            if r in (2, 3):
                pre[z * 128 : (z + 1) * 128, (r - 2) * 128 : (r - 1) * 128] = value
            kept = jnp.where(inside, jnp.where(value > 0, value, SLOPE * value), 0.0)
            hid[z * 128 : (z + 1) * 128, r * 128 : (r + 1) * 128] = kept.astype(BF16)

    held = {}
    for z in range(4):
        values = conv_plane(w_two, hid, z, 4, 0)
        for r, value in enumerate(values):
            at = (slice(z * 128, (z + 1) * 128), slice(r * 128, (r + 1) * 128))
            error = cot[at] * jnp.where(value > 0, 1.0, SLOPE)
            err[at] = error.astype(BF16)
            if r in (1, 2):
                put_errors(shifted, error, core, z, r - 1)
        own = jnp.where(core == 0, values[1], values[2])
        held[z % 2] = jnp.where(own > 0, own, SLOPE * own).reshape(16, 8, 128)
        if z % 2:
            low = low_half((16, 8, 128))
            half = slice((z // 2) * 8, (z // 2) * 8 + 8)
            for c, tile in enumerate((
                jnp.where(low, held[0], swap_halves(held[1])),
                jnp.where(low, swap_halves(held[0]), held[1]),
            )):
                out_tiles[:, c, half] = tile.astype(BF16)

    for x in range(4):
        for g in range(2):
            grads[x, 3, g * 7 + 6] = jnp.zeros((16, 128), BF16)
    tap_grad(shifted, hid, 1, total, grads, 1)

    for z in range(4):
        for r, value in enumerate(conv_plane(w_back, err, z, 2, 0)):
            slope = jnp.where(
                pre[z * 128 : (z + 1) * 128, r * 128 : (r + 1) * 128] > 0, 1.0, SLOPE
            )
            put_errors(shifted, value * slope, core, z, r)
    tap_grad(shifted, act, 2, total, grads, 0)


def compute(place, mine, other):
    vmem = pl.BlockSpec(memory_space=pltpu.VMEM)
    return pl.pallas_call(
        work,
        out_shape=(
            jax.ShapeDtypeStruct((16, 2, 16, 128), BF16),
            jax.ShapeDtypeStruct((4, 4, 14, 16, 128), BF16),
        ),
        in_specs=[pl.BlockSpec(memory_space=pltpu.SMEM), vmem, vmem],
        out_specs=(vmem, vmem),
        scratch_shapes=[
            pltpu.VMEM((512, 1024), BF16),
            pltpu.VMEM((512, 768), BF16),
            pltpu.VMEM((512, 512), BF16),
            pltpu.VMEM((512, 512), F32),
            pltpu.VMEM((3, 384, 384), BF16),
            pltpu.VMEM((3, 384, 384), BF16),
            pltpu.VMEM((3, 384, 384), BF16),
            pltpu.VMEM((512, 256), F32),
            pltpu.VMEM((192, 1024), BF16),
            pltpu.VMEM((192, 384), F32),
        ],
        compiler_params=pltpu.CompilerParams(vmem_limit_bytes=48 * 1024 * 1024),
        cost_estimate=pl.CostEstimate(flops=6_300_000_000, bytes_accessed=6_000_000, transcendentals=0),
        name="convolutions",
    )(place, mine, other)


def spread_rows(array, before, count):
    rows = jnp.transpose(array[0], (2, 1, 0, 3)).reshape(32, 16, 128)
    after = 2 * (15 + count) - 32 - before
    pairs = jnp.pad(rows, ((before, after), (0, 0), (0, 0))).reshape(15 + count, 2, 16, 128)
    return jnp.concatenate([pairs[j : j + 16] for j in range(count)], 1)


def own_taps(weight):
    rows = jnp.transpose(weight.reshape(27, 128, 4), (0, 2, 1))
    return jnp.pad(rows, ((0, 1), (0, 0), (0, 0))).reshape(7, 16, 128)


def on_device(activations, weight_one, weight_two, grad_out):
    core = lax.axis_index("c")
    chip = lax.axis_index(CHIPS)
    weights = jnp.concatenate([own_taps(weight_one), own_taps(weight_two)], 0)
    packed = jnp.concatenate(
        [
            spread_rows(activations, 3, 4),
            spread_rows(grad_out, 1, 2),
            jnp.broadcast_to(weights[None], (16, 14, 16, 128)),
        ],
        1,
    )
    mine = lax.all_to_all(packed, CHIPS, split_axis=0, concat_axis=0, tiled=True)
    other = lax.ppermute(mine, "c", [(0, 1), (1, 0)])
    place = jnp.stack([core, chip]).astype(jnp.int32)
    tiles, grads = compute(place, mine, other)

    parts = lax.all_to_all(grads.reshape(16, 14, 16, 128), ("x", "y"), split_axis=0, concat_axis=0, tiled=True)
    summed = parts.astype(F32).sum(0).astype(BF16)
    pieces = jnp.transpose(summed.reshape(14, 4, 4, 128), (1, 0, 2, 3)).reshape(1, 4, 56, 128)
    spread = jnp.broadcast_to(pieces, (4, 4, 56, 128)).reshape(16, 56, 128)
    depth = lax.all_to_all(spread, ("zh", "zl"), split_axis=0, concat_axis=0, tiled=True)
    piece = depth.astype(F32).sum(0).astype(BF16)
    every = lax.all_to_all(
        jnp.broadcast_to(piece[None], (4, 56, 128)), "y", split_axis=0, concat_axis=0, tiled=True
    )
    taps = jnp.transpose(every.reshape(4, 2, 7, 4, 128), (1, 0, 2, 3, 4)).reshape(2, 28, 4, 128)
    taps = jnp.transpose(taps[:, :27].astype(F32), (0, 1, 3, 2)).reshape(2, 3, 3, 3, 128, 4)

    rows = lax.all_to_all(tiles.reshape(32, 16, 128), FILT, split_axis=0, concat_axis=0, tiled=True)
    result = jnp.transpose(rows.reshape(32, 4, 4, 128), (2, 1, 0, 3))[None]
    return (result, taps[0], taps[1])


def solution(mesh):
    fine = Mesh(np.asarray(mesh.devices).reshape(4, 4, 2, 4, 4), ("zl", "x", "c", "zh", "y"))
    volumes = P(DP, FILT, None, None, None)
    filters = P(None, None, None, None, FILT)
    return jax.shard_map(
        on_device,
        mesh=fine,
        in_specs=(volumes, filters, filters, volumes),
        out_specs=(volumes, filters, filters),
        check_vma=False,
    )
```

```python
import jax
import jax.numpy as jnp
import numpy as np
from jax import lax
from jax.experimental import pallas as pl
from jax.experimental.pallas import tpu as pltpu
from jax.sharding import Mesh, PartitionSpec as P

SLOPE = 0.3
CHIPS = ("zl", "x")
FILT = ("zl", "x", "c")
DP = ("zh", "y")
F32 = jnp.float32
BF16 = jnp.bfloat16
ROWS, COTS, TAPS = 8, 4, 28


def low_half(shape):
    return lax.broadcasted_iota(jnp.int32, shape, len(shape) - 2) < 4


def swap_halves(tiles):
    return pltpu.roll(tiles, 4, tiles.ndim - 2)


def merge(even, odd):
    low = low_half(even.shape)
    return jnp.where(low, even, swap_halves(odd)), jnp.where(low, swap_halves(even), odd)


def shift_lanes(block, by):
    lane = lax.broadcasted_iota(jnp.int32, block.shape, 1)
    edge = 0 if by > 0 else 127
    return jnp.where(lane == edge, 0.0, pltpu.roll(block, by % 128, 1))


def conv_plane(weights, source, depth, rows, first_row):
    low, high = max(depth - 1, 0), min(depth + 1, 3)
    taps = slice((low - depth + 1) * 128, (high - depth + 2) * 128)
    total = None
    for b in range(3):
        lanes = slice((first_row + b) * 128, (first_row + b + rows) * 128)
        part = jnp.dot(
            weights[b, :, taps],
            source[low * 128 : (high + 1) * 128, lanes],
            preferred_element_type=F32,
        )
        total = part if total is None else total + part
    out = []
    for r in range(rows):
        block = total[:, r * 128 : (r + 1) * 128]
        out.append(
            block[128:256] + shift_lanes(block[:128], 1) + shift_lanes(block[256:], -1)
        )
    return out


def own_rows(block, core):
    tiles = pltpu.roll(block.reshape(4, 4, 8, 128), (8 - 4 * core) % 8, 2)
    pairs = []
    for x in range(4):
        for zl in (0, 2):
            one, two = tiles[zl, x], tiles[zl + 1, x]
            pairs.append(jnp.where(low_half(one.shape), one, swap_halves(two)))
    return jnp.concatenate(pairs, 0)


def put_errors(shifted, block, core, depth, row):
    own = own_rows(block, core)
    lanes = slice((depth * 2 + row) * 128, (depth * 2 + row + 1) * 128)
    shifted[0:64, lanes] = shift_lanes(own, -1).astype(BF16)
    shifted[64:128, lanes] = own.astype(BF16)
    shifted[128:192, lanes] = shift_lanes(own, 1).astype(BF16)


def tap_grad(shifted, source, first_row, total, out, which):
    for b in range(3):
        lanes = slice((first_row + b) * 128, (first_row + b + 2) * 128)
        total[...] = jnp.zeros_like(total)
        for depth in range(4):
            low, high = max(depth - 1, 0), min(depth + 1, 3)
            taps = slice((low - depth + 1) * 128, (high - depth + 2) * 128)
            total[:, taps] += lax.dot_general(
                shifted[:, depth * 256 : (depth + 1) * 256],
                source[low * 128 : (high + 1) * 128, lanes],
                (((1,), (1,)), ((), ())),
                preferred_element_type=F32,
            )
        for a in range(3):
            for e in range(3):
                tap = a * 9 + b * 3 + e
                for x in range(4):
                    out[x, tap // 7, which * 7 + tap % 7] = total[
                        e * 64 + x * 16 : e * 64 + (x + 1) * 16, a * 128 : (a + 1) * 128
                    ].astype(BF16)


def work(
    place, mine, other, mine_taps, other_taps, out_tiles, grads,
    act, hid, err, cot, w_one, w_two, w_back, pre, shifted, total, tiles, sent,
):
    core, chip = place[0], place[1]

    even_core = lax.broadcast(core, (16, 2, 8, 128)) == 0

    def load(one, two):
        one = one.astype(F32).reshape(16, 2, 8, 128)
        two = two.astype(F32).reshape(16, 2, 8, 128)
        return jnp.where(even_core, one, two), jnp.where(even_core, two, one)

    def filters(source, step):
        return jnp.stack([source[x, zl, step] for zl in range(4) for x in range(4)])

    def planes(one, two, h):
        merged = merge(one[:, h], two[:, h])
        return [plane.reshape(128, 128) for plane in merged]

    for r in range(ROWS):
        one, two = load(mine[:, r], other[:, r])
        for h in range(2):
            for p, plane in enumerate(planes(one, two, h)):
                z = 2 * h + p
                act[z * 128 : (z + 1) * 128, r * 128 : (r + 1) * 128] = plane.astype(BF16)
    for layer in range(2):
        for step in range(7):
            at = layer * 7 + step
            one, two = load(filters(mine_taps, at), filters(other_taps, at))
            for h in range(2):
                for p, plane in enumerate(planes(one, two, h)):
                    tap = 4 * step + 2 * h + p
                    if tap >= 27:
                        continue
                    a, b, e = tap // 9, tap // 3 % 3, tap % 3
                    into = w_two if layer else w_one
                    into[b, e * 128 : (e + 1) * 128, a * 128 : (a + 1) * 128] = plane.astype(BF16)
                    if layer:
                        a, b, e = 2 - a, 2 - b, 2 - e
                        w_back[b, e * 128 : (e + 1) * 128, a * 128 : (a + 1) * 128] = plane.T.astype(BF16)
    for r in range(COTS):
        one, two = load(mine[:, ROWS + r], other[:, ROWS + r])
        for h in range(2):
            for p, plane in enumerate(planes(one, two, h)):
                z = 2 * h + p
                cot[z * 128 : (z + 1) * 128, r * 128 : (r + 1) * 128] = plane

    for z in range(4):
        for r, value in enumerate(conv_plane(w_one, act, z, 6, 0)):
            row = 2 * chip - 2 + r
            inside = jnp.logical_and(row >= 0, row < 32)
            if r in (2, 3):
                pre[z * 128 : (z + 1) * 128, (r - 2) * 128 : (r - 1) * 128] = value
            kept = jnp.where(inside, jnp.where(value > 0, value, SLOPE * value), 0.0)
            hid[z * 128 : (z + 1) * 128, r * 128 : (r + 1) * 128] = kept.astype(BF16)

    held = {}
    for z in range(4):
        values = conv_plane(w_two, hid, z, 4, 0)
        for r, value in enumerate(values):
            at = (slice(z * 128, (z + 1) * 128), slice(r * 128, (r + 1) * 128))
            error = cot[at] * jnp.where(value > 0, 1.0, SLOPE)
            err[at] = error.astype(BF16)
            if r in (1, 2):
                put_errors(shifted, error, core, z, r - 1)
        own = jnp.where(core == 0, values[1], values[2])
        held[z % 2] = jnp.where(own > 0, own, SLOPE * own).reshape(16, 8, 128)
        if z % 2:
            low = low_half((16, 8, 128))
            rows = slice((z // 2) * 8, (z // 2) * 8 + 8)
            for c, tile in enumerate((
                jnp.where(low, held[0], swap_halves(held[1])),
                jnp.where(low, swap_halves(held[0]), held[1]),
            )):
                tiles[:, c, rows] = tile.astype(BF16)
    send = pltpu.make_async_copy(tiles, out_tiles, sent)
    send.start()

    for x in range(4):
        for g in range(2):
            grads[x, 3, g * 7 + 6] = jnp.zeros((16, 128), BF16)
    tap_grad(shifted, hid, 1, total, grads, 1)

    for z in range(4):
        for r, value in enumerate(conv_plane(w_back, err, z, 2, 0)):
            slope = jnp.where(
                pre[z * 128 : (z + 1) * 128, r * 128 : (r + 1) * 128] > 0, 1.0, SLOPE
            )
            put_errors(shifted, value * slope, core, z, r)
    tap_grad(shifted, act, 2, total, grads, 0)
    send.wait()


def compute(place, *arrays):
    vmem = pl.BlockSpec(memory_space=pltpu.VMEM)
    return pl.pallas_call(
        work,
        out_shape=(
            jax.ShapeDtypeStruct((16, 2, 16, 128), BF16),
            jax.ShapeDtypeStruct((4, 4, 14, 16, 128), BF16),
        ),
        in_specs=[pl.BlockSpec(memory_space=pltpu.SMEM), vmem, vmem, vmem, vmem],
        out_specs=(pl.BlockSpec(memory_space=pltpu.HBM), vmem),
        scratch_shapes=[
            pltpu.VMEM((512, 1024), BF16),
            pltpu.VMEM((512, 768), BF16),
            pltpu.VMEM((512, 512), BF16),
            pltpu.VMEM((512, 512), F32),
            pltpu.VMEM((3, 384, 384), BF16),
            pltpu.VMEM((3, 384, 384), BF16),
            pltpu.VMEM((3, 384, 384), BF16),
            pltpu.VMEM((512, 256), F32),
            pltpu.VMEM((192, 1024), BF16),
            pltpu.VMEM((192, 384), F32),
            pltpu.VMEM((16, 2, 16, 128), BF16),
            pltpu.SemaphoreType.DMA,
        ],
        compiler_params=pltpu.CompilerParams(vmem_limit_bytes=48 * 1024 * 1024),
        cost_estimate=pl.CostEstimate(flops=6_300_000_000, bytes_accessed=6_000_000, transcendentals=0),
        name="convolutions",
    )(place, *arrays)


def pack_taps(one, two, out, near, sems):
    copies = [pltpu.make_async_copy(taps, near.at[n], sems.at[n]) for n, taps in enumerate((one, two))]
    for copy in copies:
        copy.start()
    for layer, copy in enumerate(copies):
        copy.wait()
        for step in range(7):
            parts = [near[layer, 4 * step + t].astype(F32) for t in range(min(4, 27 - 4 * step))]
            if len(parts) == 3:
                parts.append(jnp.zeros((4, 128), F32))
            tile = jnp.concatenate(parts, 0).astype(BF16)
            for zl in range(4):
                out[zl, layer * 7 + step] = tile


def pack_rows(volume, cotangent, after, out):
    for source, start, halo, count in ((volume, 0, 3, ROWS), (cotangent, ROWS, 1, COTS)):
        planes = [source[ch, z].astype(F32) for z in range(4) for ch in range(4)]
        rows = jnp.swapaxes(jnp.stack(planes), 0, 1).astype(BF16)
        for chip in range(16):
            for r in range(count):
                row = 2 * chip + r - halo
                if 0 <= row < 32:
                    out[chip, start + r] = rows[row]
                else:
                    out[chip, start + r] = jnp.zeros((16, 128), BF16)


def sum_pieces(pieces, tiles, total, kept):
    total[...] = pieces[...].astype(F32).sum(0).astype(BF16)


VMEM = pl.BlockSpec(memory_space=pltpu.VMEM)
HBM = pl.BlockSpec(memory_space=pltpu.HBM)


def on_chip(kernel, shapes, specs, *arrays, out_specs=VMEM, **options):
    return pl.pallas_call(
        kernel,
        out_shape=shapes,
        in_specs=specs,
        out_specs=out_specs,
        compiler_params=pltpu.CompilerParams(vmem_limit_bytes=24 * 1024 * 1024),
        **options,
    )(*arrays)


def own_taps(weight):
    return jnp.transpose(weight.reshape(27, 128, 4), (0, 2, 1))


def exchange(array, axis):
    return lax.all_to_all(array, axis, split_axis=0, concat_axis=0, tiled=True)


def on_device(activations, weight_one, weight_two, grad_out):
    core = lax.axis_index("c")
    chip = lax.axis_index(CHIPS)
    taps = on_chip(
        pack_taps, jax.ShapeDtypeStruct((4, 14, 16, 128), BF16), [HBM, HBM],
        own_taps(weight_one), own_taps(weight_two),
        scratch_shapes=[pltpu.VMEM((2, 27, 4, 128), BF16), pltpu.SemaphoreType.DMA((2,))],
        name="pack_taps",
    )
    line = exchange(taps, "zl")
    packed = on_chip(
        pack_rows, jax.ShapeDtypeStruct((16, ROWS + COTS, 16, 128), BF16), [VMEM, VMEM, HBM],
        activations[0], grad_out[0], line, name="pack_rows",
    )
    mine = exchange(packed, CHIPS)
    mine_taps = lax.all_gather(line[None], "x", axis=0, tiled=True)
    swap = [(0, 1), (1, 0)]
    other, other_taps = lax.ppermute(mine, "c", swap), lax.ppermute(mine_taps, "c", swap)
    place = jnp.stack([core, chip]).astype(jnp.int32)
    tiles, grads = compute(place, mine, other, mine_taps, other_taps)

    parts = exchange(grads.reshape(16, 14, 16, 128), ("x", "y"))
    summed = parts.astype(F32).sum(0).astype(BF16)
    pieces = jnp.transpose(summed.reshape(14, 4, 4, 128), (1, 0, 2, 3)).reshape(1, 4, 56, 128)
    spread = jnp.broadcast_to(pieces, (4, 4, 56, 128)).reshape(16, 56, 128)
    depth = exchange(spread, ("zh", "zl"))

    piece, tiles = on_chip(
        sum_pieces,
        (jax.ShapeDtypeStruct((56, 128), BF16), jax.ShapeDtypeStruct(tiles.shape, BF16)),
        [VMEM, HBM], depth, tiles,
        out_specs=(VMEM, HBM),
        input_output_aliases={1: 1},
        name="sum_pieces",
    )
    every = lax.all_gather(piece[None], "y", axis=0, tiled=True)
    found = jnp.transpose(every.reshape(4, 2, 7, 4, 128), (1, 0, 2, 3, 4)).reshape(2, 28, 4, 128)
    found = jnp.transpose(found[:, :27].astype(F32), (0, 1, 3, 2)).reshape(2, 3, 3, 3, 128, 4)

    rows = exchange(tiles.reshape(32, 16, 128), FILT)
    result = jnp.transpose(rows.reshape(32, 4, 4, 128), (2, 1, 0, 3))[None]
    return (result, found[0], found[1])


def solution(mesh):
    fine = Mesh(np.asarray(mesh.devices).reshape(4, 4, 2, 4, 4), ("zl", "x", "c", "zh", "y"))
    volumes = P(DP, FILT, None, None, None)
    filters = P(None, None, None, None, FILT)
    return jax.shard_map(
        on_device,
        mesh=fine,
        in_specs=(volumes, filters, filters, volumes),
        out_specs=(volumes, filters, filters),
        check_vma=False,
    )
```

```python
import jax
import jax.numpy as jnp
import numpy as np
from jax import lax
from jax.experimental import pallas as pl
from jax.experimental.pallas import tpu as pltpu
from jax.sharding import Mesh, PartitionSpec as P

SLOPE = 0.3
CHIPS = ("zl", "x")
FILT = ("zl", "x", "c")
DP = ("zh", "y")
F32 = jnp.float32
BF16 = jnp.bfloat16
ROWS, COTS, TAPS = 8, 4, 28


def low_half(shape):
    return lax.broadcasted_iota(jnp.int32, shape, len(shape) - 2) < 4


def swap_halves(tiles):
    return pltpu.roll(tiles, 4, tiles.ndim - 2)


def channel_order():
    row = lax.broadcasted_iota(jnp.int32, (128, 128), 0)
    column = lax.broadcasted_iota(jnp.int32, (128, 128), 1)
    core, x, zl, last = column // 64, column // 16 % 4, column // 4 % 4, column % 4
    return jnp.where(row == 32 * zl + 8 * x + 4 * core + last, 1.0, 0.0).astype(BF16)


def merge(even, odd):
    low = low_half(even.shape)
    return jnp.where(low, even, swap_halves(odd)), jnp.where(low, swap_halves(even), odd)


def shift_lanes(block, by):
    lane = lax.broadcasted_iota(jnp.int32, block.shape, 1)
    edge = 0 if by > 0 else 127
    return jnp.where(lane == edge, 0.0, pltpu.roll(block, by % 128, 1))


def conv_plane(weights, source, depth, rows, first_row):
    low, high = max(depth - 1, 0), min(depth + 1, 3)
    taps = slice((low - depth + 1) * 128, (high - depth + 2) * 128)
    total = jnp.dot(
        jnp.concatenate([weights[b, :, taps] for b in range(3)], 1),
        jnp.concatenate([
            source[low * 128 : (high + 1) * 128, (first_row + b) * 128 : (first_row + b + rows) * 128]
            for b in range(3)
        ], 0),
        preferred_element_type=F32,
    )
    out = []
    for r in range(rows):
        block = total[:, r * 128 : (r + 1) * 128]
        out.append(
            block[128:256] + shift_lanes(block[:128], 1) + shift_lanes(block[256:], -1)
        )
    return out


def put_errors(shifted, block, core, depth, row):
    own = jnp.where(core == 0, block[:64], block[64:])
    lanes = slice((depth * 2 + row) * 128, (depth * 2 + row + 1) * 128)
    shifted[0:64, lanes] = shift_lanes(own, -1).astype(BF16)
    shifted[64:128, lanes] = own.astype(BF16)
    shifted[128:192, lanes] = shift_lanes(own, 1).astype(BF16)


def tap_grad(shifted, source, first_row, total, out, which):
    for b in range(3):
        lanes = slice((first_row + b) * 128, (first_row + b + 2) * 128)
        total[...] = jnp.zeros_like(total)
        for depth in range(4):
            low, high = max(depth - 1, 0), min(depth + 1, 3)
            taps = slice((low - depth + 1) * 128, (high - depth + 2) * 128)
            total[:, taps] += lax.dot_general(
                shifted[:, depth * 256 : (depth + 1) * 256],
                source[low * 128 : (high + 1) * 128, lanes],
                (((1,), (1,)), ((), ())),
                preferred_element_type=F32,
            )
        for a in range(3):
            for e in range(3):
                tap = a * 9 + b * 3 + e
                for x in range(4):
                    out[x, tap // 7, which * 7 + tap % 7] = total[
                        e * 64 + x * 16 : e * 64 + (x + 1) * 16, a * 128 : (a + 1) * 128
                    ].astype(BF16)


def planes(group, h):
    halves = [[tile.astype(F32)[h * 8 : h * 8 + 8] for tile in line] for line in group]
    even = jnp.stack([line[zl] for line in halves for zl in (0, 2)])
    odd = jnp.stack([line[zl] for line in halves for zl in (1, 3)])
    return [plane.reshape(64, 128).astype(BF16) for plane in merge(even, odd)]


def place_half(side, rows, taps, act, cot, w_one, w_two):
    def rows_of(first):
        return pl.ds(pl.multiple_of(first + 64 * side, 64), 64)

    for layer, into in enumerate((w_one, w_two)):
        for step in range(7):
            group = [[taps[x, zl, layer * 7 + step] for zl in range(4)] for x in range(4)]
            for h in range(2):
                for p, plane in enumerate(planes(group, h)):
                    tap = 4 * step + 2 * h + p
                    if tap < 27:
                        a, b, e = tap // 9, tap // 3 % 3, tap % 3
                        into[b, rows_of(e * 128), a * 128 : (a + 1) * 128] = plane
    for first, count, into in ((0, ROWS, act), (ROWS, COTS, cot)):
        for r in range(count):
            group = [[rows[zl * 4 + x, first + r] for zl in range(4)] for x in range(4)]
            for h in range(2):
                for p, plane in enumerate(planes(group, h)):
                    into[rows_of((2 * h + p) * 128), r * 128 : (r + 1) * 128] = plane


def place_mine(place, mine, taps, act, cot, w_one, w_two):
    place_half(place[0], mine, taps, act, cot, w_one, w_two)


def work(
    place, far, other_taps, act_in, cot_in, one_in, two_in,
    out_tiles, grads, act, cot, w_one, w_two,
    hid, err, w_back, pre, shifted, total, tiles, sent,
):
    core, chip = place[0], place[1]
    place_half(1 - core, far, other_taps, act, cot, w_one, w_two)
    for a in range(3):
        for b in range(3):
            for e in range(3):
                block = w_two[b, e * 128 : (e + 1) * 128, a * 128 : (a + 1) * 128]
                w_back[2 - b, (2 - e) * 128 : (3 - e) * 128, (2 - a) * 128 : (3 - a) * 128] = block.T

    for z in range(4):
        for r, value in enumerate(conv_plane(w_one, act, z, 6, 0)):
            row = 2 * chip - 2 + r
            inside = jnp.logical_and(row >= 0, row < 32)
            if r in (2, 3):
                pre[z * 128 : (z + 1) * 128, (r - 2) * 128 : (r - 1) * 128] = value
            kept = jnp.where(inside, jnp.where(value > 0, value, SLOPE * value), 0.0)
            hid[z * 128 : (z + 1) * 128, r * 128 : (r + 1) * 128] = kept.astype(BF16)

    held = {}
    for z in range(4):
        values = conv_plane(w_two, hid, z, 4, 0)
        for r, value in enumerate(values):
            at = (slice(z * 128, (z + 1) * 128), slice(r * 128, (r + 1) * 128))
            error = cot[at].astype(F32) * jnp.where(value > 0, 1.0, SLOPE)
            err[at] = error.astype(BF16)
            if r in (1, 2):
                put_errors(shifted, error, core, z, r - 1)
        own = jnp.where(core == 0, values[1], values[2])
        held[z % 2] = jnp.where(own > 0, own, SLOPE * own).reshape(2, 4, 2, 8, 128)
        if z % 2:
            half = slice((z // 2) * 8, (z // 2) * 8 + 8)
            for odd, tile in enumerate(merge(held[0], held[1])):
                for c in range(2):
                    for x in range(4):
                        for pair in range(2):
                            tiles[(2 * pair + odd) * 4 + x, c, half] = tile[c, x, pair].astype(BF16)
    send = pltpu.make_async_copy(tiles, out_tiles, sent)
    send.start()

    for x in range(4):
        for g in range(2):
            grads[x, 3, g * 7 + 6] = jnp.zeros((16, 128), BF16)
    tap_grad(shifted, hid, 1, total, grads, 1)

    for z in range(4):
        for r, value in enumerate(conv_plane(w_back, err, z, 2, 0)):
            slope = jnp.where(
                pre[z * 128 : (z + 1) * 128, r * 128 : (r + 1) * 128] > 0, 1.0, SLOPE
            )
            put_errors(shifted, value * slope, core, z, r)
    tap_grad(shifted, act, 2, total, grads, 0)
    send.wait()


def compute(place, mine, far, mine_taps, other_taps):
    smem = pl.BlockSpec(memory_space=pltpu.SMEM)
    halves = (
        jax.ShapeDtypeStruct((512, ROWS * 128), BF16),
        jax.ShapeDtypeStruct((512, COTS * 128), BF16),
        jax.ShapeDtypeStruct((3, 384, 384), BF16),
        jax.ShapeDtypeStruct((3, 384, 384), BF16),
    )
    half = on_chip(
        place_mine, halves, [smem, VMEM, VMEM], place, mine, mine_taps, out_specs=(VMEM,) * 4, name="place_mine"
    )
    tiles, grads, *_ = on_chip(
        work,
        (
            jax.ShapeDtypeStruct((16, 2, 16, 128), BF16),
            jax.ShapeDtypeStruct((4, 4, 14, 16, 128), BF16),
            *halves,
        ),
        [smem] + [VMEM] * 6, place, far, other_taps, *half,
        out_specs=(HBM,) + (VMEM,) * 5,
        input_output_aliases={3: 2, 4: 3, 5: 4, 6: 5},
        scratch_shapes=[
            pltpu.VMEM((512, 768), BF16),
            pltpu.VMEM((512, 512), BF16),
            pltpu.VMEM((3, 384, 384), BF16),
            pltpu.VMEM((512, 256), F32),
            pltpu.VMEM((192, 1024), BF16),
            pltpu.VMEM((192, 384), F32),
            pltpu.VMEM((16, 2, 16, 128), BF16),
            pltpu.SemaphoreType.DMA,
        ],
        cost_estimate=pl.CostEstimate(flops=6_300_000_000, bytes_accessed=6_000_000, transcendentals=0),
        name="convolutions",
    )
    return tiles, grads


def pack_taps(one, two, out, near, sems):
    copies = [pltpu.make_async_copy(taps, near.at[n], sems.at[n]) for n, taps in enumerate((one, two))]
    for copy in copies:
        copy.start()
    order = channel_order()
    for layer, copy in enumerate(copies):
        copy.wait()
        for step in range(7):
            parts = [near[layer, 4 * step + t].astype(F32) for t in range(min(4, 27 - 4 * step))]
            if len(parts) == 3:
                parts.append(jnp.zeros((4, 128), F32))
            tile = jnp.concatenate(parts, 0).astype(BF16)
            tile = jnp.dot(tile, order, preferred_element_type=F32).astype(BF16)
            for zl in range(4):
                out[zl, layer * 7 + step] = tile


def pack_rows(volume, cotangent, out, near, sems):
    for source, start, halo, count in ((volume, 0, 3, ROWS), (cotangent, ROWS, 1, COTS)):
        planes = [source[ch, z].astype(F32) for z in range(4) for ch in range(4)]
        rows = jnp.swapaxes(jnp.stack(planes), 0, 1).astype(BF16)
        for chip in range(16):
            for r in range(count):
                row = 2 * chip + r - halo
                if 0 <= row < 32:
                    near[chip, start + r] = rows[row]
                else:
                    near[chip, start + r] = jnp.zeros((16, 128), BF16)
    copies = [pltpu.make_async_copy(near.at[chip], out.at[chip], sems.at[chip]) for chip in range(16)]
    for copy in copies:
        copy.start()
    for copy in copies:
        copy.wait()


def hold(packed, after, out):
    pass


def sum_pieces(pieces, tiles, total, kept):
    found = pieces[...].astype(F32).sum(0).astype(BF16)
    total[...] = lax.dot_general(
        found, channel_order(), (((1,), (1,)), ((), ())), preferred_element_type=F32
    ).astype(BF16)


VMEM = pl.BlockSpec(memory_space=pltpu.VMEM)
HBM = pl.BlockSpec(memory_space=pltpu.HBM)


def on_chip(kernel, shapes, specs, *arrays, out_specs=VMEM, room=24, **options):
    return pl.pallas_call(
        kernel,
        out_shape=shapes,
        in_specs=specs,
        out_specs=out_specs,
        compiler_params=pltpu.CompilerParams(vmem_limit_bytes=room * 1024 * 1024),
        **options,
    )(*arrays)


def own_taps(weight):
    return jnp.transpose(weight.reshape(27, 128, 4), (0, 2, 1))


def exchange(array, axis):
    return lax.all_to_all(array, axis, split_axis=0, concat_axis=0, tiled=True)


def on_device(activations, weight_one, weight_two, grad_out):
    core = lax.axis_index("c")
    chip = lax.axis_index(CHIPS)
    taps = on_chip(
        pack_taps, jax.ShapeDtypeStruct((4, 14, 16, 128), BF16), [HBM, HBM],
        own_taps(weight_one), own_taps(weight_two),
        scratch_shapes=[pltpu.VMEM((2, 27, 4, 128), BF16), pltpu.SemaphoreType.DMA((2,))],
        room=60, name="pack_taps",
    )
    line = exchange(taps, "zl")
    packed = on_chip(
        pack_rows, jax.ShapeDtypeStruct((16, ROWS + COTS, 16, 128), BF16), [VMEM, VMEM],
        activations[0], grad_out[0], out_specs=HBM, scratch_shapes=[
            pltpu.VMEM((16, ROWS + COTS, 16, 128), BF16), pltpu.SemaphoreType.DMA((16,)),
        ],
        name="pack_rows",
    )
    packed = on_chip(
        hold, jax.ShapeDtypeStruct(packed.shape, BF16), [HBM, HBM], packed, line,
        out_specs=HBM, input_output_aliases={0: 0}, name="hold",
    )
    mine = exchange(packed, CHIPS)
    mine_taps = lax.all_gather(line[None], "x", axis=0, tiled=True)
    swap = [(0, 1), (1, 0)]
    other, other_taps = lax.ppermute(mine, "c", swap), lax.ppermute(mine_taps, "c", swap)
    place = jnp.stack([core, chip]).astype(jnp.int32)
    tiles, grads = compute(place, mine, other, mine_taps, other_taps)

    parts = exchange(grads.reshape(16, 14, 16, 128), ("x", "y"))
    summed = parts.astype(F32).sum(0).astype(BF16)
    pieces = jnp.transpose(summed.reshape(14, 4, 4, 128), (1, 0, 2, 3)).reshape(1, 4, 56, 128)
    spread = jnp.broadcast_to(pieces, (4, 4, 56, 128)).reshape(16, 56, 128)
    depth = exchange(spread, ("zh", "zl"))

    piece, tiles = on_chip(
        sum_pieces,
        (jax.ShapeDtypeStruct((56, 128), BF16), jax.ShapeDtypeStruct(tiles.shape, BF16)),
        [VMEM, HBM], depth, tiles,
        out_specs=(VMEM, HBM),
        input_output_aliases={1: 1},
        name="sum_pieces",
    )
    every = lax.all_gather(piece[None], "y", axis=0, tiled=True)
    found = jnp.transpose(every.reshape(4, 2, 7, 4, 128), (1, 0, 2, 3, 4)).reshape(2, 28, 4, 128)
    found = jnp.transpose(found[:, :27].astype(F32), (0, 1, 3, 2)).reshape(2, 3, 3, 3, 128, 4)

    rows = exchange(tiles.reshape(32, 16, 128), FILT)
    result = jnp.transpose(rows.reshape(32, 4, 4, 128), (2, 1, 0, 3))[None]
    return (result, found[0], found[1])


def solution(mesh):
    fine = Mesh(np.asarray(mesh.devices).reshape(4, 4, 2, 4, 4), ("zl", "x", "c", "zh", "y"))
    volumes = P(DP, FILT, None, None, None)
    filters = P(None, None, None, None, FILT)
    return jax.shard_map(
        on_device,
        mesh=fine,
        in_specs=(volumes, filters, filters, volumes),
        out_specs=(volumes, filters, filters),
        check_vma=False,
    )
```

```python
import jax
import jax.numpy as jnp
import numpy as np
from jax import lax
from jax.experimental import pallas as pl
from jax.experimental.pallas import tpu as pltpu
from jax.sharding import Mesh, PartitionSpec as P

SLOPE = 0.3
CHIPS = ("zl", "x")
FILT = ("zl", "x", "c")
DP = ("zh", "y")
F32 = jnp.float32
BF16 = jnp.bfloat16
ROWS, COTS, TAPS = 8, 4, 28


def low_half(shape):
    return lax.broadcasted_iota(jnp.int32, shape, len(shape) - 2) < 4


def swap_halves(tiles):
    return pltpu.roll(tiles, 4, tiles.ndim - 2)


def channel_order():
    row = lax.broadcasted_iota(jnp.int32, (128, 128), 0)
    column = lax.broadcasted_iota(jnp.int32, (128, 128), 1)
    core, x, zl, last = column // 64, column // 16 % 4, column // 4 % 4, column % 4
    return jnp.where(row == 32 * zl + 8 * x + 4 * core + last, 1.0, 0.0).astype(BF16)


def merge(even, odd):
    low = low_half(even.shape)
    return jnp.where(low, even, swap_halves(odd)), jnp.where(low, swap_halves(even), odd)


def shift_lanes(block, by):
    lane = lax.broadcasted_iota(jnp.int32, block.shape, 1)
    edge = 0 if by > 0 else 127
    return jnp.where(lane == edge, 0.0, pltpu.roll(block, by % 128, 1))


def conv_plane(weights, source, depth, rows, first_row):
    low, high = max(depth - 1, 0), min(depth + 1, 3)
    taps = slice((low - depth + 1) * 128, (high - depth + 2) * 128)
    total = jnp.dot(
        jnp.concatenate([weights[b, :, taps] for b in range(3)], 1),
        jnp.concatenate([
            source[low * 128 : (high + 1) * 128, (first_row + b) * 128 : (first_row + b + rows) * 128]
            for b in range(3)
        ], 0),
        preferred_element_type=F32,
    )
    out = []
    for r in range(rows):
        block = total[:, r * 128 : (r + 1) * 128]
        out.append(
            block[128:256] + shift_lanes(block[:128], 1) + shift_lanes(block[256:], -1)
        )
    return out


def put_errors(shifted, block, core, depth, row):
    own = jnp.where(core == 0, block[:64], block[64:])
    lanes = slice((depth * 2 + row) * 128, (depth * 2 + row + 1) * 128)
    shifted[0:64, lanes] = shift_lanes(own, -1).astype(BF16)
    shifted[64:128, lanes] = own.astype(BF16)
    shifted[128:192, lanes] = shift_lanes(own, 1).astype(BF16)


def tap_grad(shifted, source, first_row, total, out, which):
    for b in range(3):
        lanes = slice((first_row + b) * 128, (first_row + b + 2) * 128)
        total[...] = jnp.zeros_like(total)
        for depth in range(4):
            low, high = max(depth - 1, 0), min(depth + 1, 3)
            taps = slice((low - depth + 1) * 128, (high - depth + 2) * 128)
            total[:, taps] += lax.dot_general(
                shifted[:, depth * 256 : (depth + 1) * 256],
                source[low * 128 : (high + 1) * 128, lanes],
                (((1,), (1,)), ((), ())),
                preferred_element_type=F32,
            )
        for a in range(3):
            for e in range(3):
                tap = a * 9 + b * 3 + e
                for x in range(4):
                    out[x, tap // 7, which * 7 + tap % 7] = total[
                        e * 64 + x * 16 : e * 64 + (x + 1) * 16, a * 128 : (a + 1) * 128
                    ].astype(BF16)


def planes(group, h):
    halves = [[tile.astype(F32)[h * 8 : h * 8 + 8] for tile in line] for line in group]
    even = jnp.stack([line[zl] for line in halves for zl in (0, 2)])
    odd = jnp.stack([line[zl] for line in halves for zl in (1, 3)])
    return [plane.reshape(64, 128).astype(BF16) for plane in merge(even, odd)]


def place_half(side, rows, taps, act, cot, w_one, w_two):
    def rows_of(first):
        return pl.ds(pl.multiple_of(first + 64 * side, 64), 64)

    for layer, into in enumerate((w_one, w_two)):
        for step in range(7):
            group = [[taps[x, zl, layer * 7 + step] for zl in range(4)] for x in range(4)]
            for h in range(2):
                for p, plane in enumerate(planes(group, h)):
                    tap = 4 * step + 2 * h + p
                    if tap < 27:
                        a, b, e = tap // 9, tap // 3 % 3, tap % 3
                        into[b, rows_of(e * 128), a * 128 : (a + 1) * 128] = plane
    for first, count, into in ((0, ROWS, act), (ROWS, COTS, cot)):
        for r in range(count):
            group = [[rows[zl * 4 + x, first + r] for zl in range(4)] for x in range(4)]
            for h in range(2):
                for p, plane in enumerate(planes(group, h)):
                    into[rows_of((2 * h + p) * 128), r * 128 : (r + 1) * 128] = plane


def place_mine(place, mine, taps, act, cot, w_one, w_two):
    place_half(place[0], mine, taps, act, cot, w_one, w_two)


def work(
    place, far, other_taps, act_in, cot_in, one_in, two_in,
    out_tiles, grads, act, cot, w_one, w_two,
    hid, err, w_back, pre, shifted, total,
):
    core, chip = place[0], place[1]
    place_half(1 - core, far, other_taps, act, cot, w_one, w_two)
    for a in range(3):
        for b in range(3):
            for e in range(3):
                block = w_two[b, e * 128 : (e + 1) * 128, a * 128 : (a + 1) * 128]
                w_back[2 - b, (2 - e) * 128 : (3 - e) * 128, (2 - a) * 128 : (3 - a) * 128] = block.T

    for z in range(4):
        for r, value in enumerate(conv_plane(w_one, act, z, 6, 0)):
            row = 2 * chip - 2 + r
            inside = jnp.logical_and(row >= 0, row < 32)
            if r in (2, 3):
                pre[z * 128 : (z + 1) * 128, (r - 2) * 128 : (r - 1) * 128] = value
            kept = jnp.where(inside, jnp.where(value > 0, value, SLOPE * value), 0.0)
            hid[z * 128 : (z + 1) * 128, r * 128 : (r + 1) * 128] = kept.astype(BF16)

    held = {}
    for z in range(4):
        values = conv_plane(w_two, hid, z, 4, 0)
        for r, value in enumerate(values):
            at = (slice(z * 128, (z + 1) * 128), slice(r * 128, (r + 1) * 128))
            error = cot[at].astype(F32) * jnp.where(value > 0, 1.0, SLOPE)
            err[at] = error.astype(BF16)
            if r in (1, 2):
                put_errors(shifted, error, core, z, r - 1)
        own = jnp.where(core == 0, values[1], values[2])
        held[z % 2] = jnp.where(own > 0, own, SLOPE * own).reshape(2, 4, 2, 8, 128)
        if z % 2:
            half = slice((z // 2) * 8, (z // 2) * 8 + 8)
            for odd, tile in enumerate(merge(held[0], held[1])):
                for c in range(2):
                    for x in range(4):
                        for pair in range(2):
                            out_tiles[(2 * pair + odd) * 4 + x, c, half] = tile[c, x, pair].astype(BF16)

    for x in range(4):
        for g in range(2):
            grads[x, 3, g * 7 + 6] = jnp.zeros((16, 128), BF16)
    tap_grad(shifted, hid, 1, total, grads, 1)

    for z in range(4):
        for r, value in enumerate(conv_plane(w_back, err, z, 2, 0)):
            slope = jnp.where(
                pre[z * 128 : (z + 1) * 128, r * 128 : (r + 1) * 128] > 0, 1.0, SLOPE
            )
            put_errors(shifted, value * slope, core, z, r)
    tap_grad(shifted, act, 2, total, grads, 0)


def compute(place, mine, far, mine_taps, other_taps):
    smem = pl.BlockSpec(memory_space=pltpu.SMEM)
    halves = (
        jax.ShapeDtypeStruct((512, ROWS * 128), BF16),
        jax.ShapeDtypeStruct((512, COTS * 128), BF16),
        jax.ShapeDtypeStruct((3, 384, 384), BF16),
        jax.ShapeDtypeStruct((3, 384, 384), BF16),
    )
    half = on_chip(
        place_mine, halves, [smem, VMEM, VMEM], place, mine, mine_taps, out_specs=(VMEM,) * 4, name="place_mine"
    )
    tiles, grads, *_ = on_chip(
        work,
        (
            jax.ShapeDtypeStruct((16, 2, 16, 128), BF16),
            jax.ShapeDtypeStruct((4, 4, 14, 16, 128), BF16),
            *halves,
        ),
        [smem] + [VMEM] * 6, place, far, other_taps, *half,
        out_specs=(VMEM,) * 6,
        input_output_aliases={3: 2, 4: 3, 5: 4, 6: 5},
        scratch_shapes=[
            pltpu.VMEM((512, 768), BF16),
            pltpu.VMEM((512, 512), BF16),
            pltpu.VMEM((3, 384, 384), BF16),
            pltpu.VMEM((512, 256), F32),
            pltpu.VMEM((192, 1024), BF16),
            pltpu.VMEM((192, 384), F32),
        ],
        cost_estimate=pl.CostEstimate(flops=6_300_000_000, bytes_accessed=6_000_000, transcendentals=0),
        name="convolutions",
    )
    return tiles, grads


def pack_taps(one, two, out, near, sems):
    copies = [pltpu.make_async_copy(taps, near.at[n], sems.at[n]) for n, taps in enumerate((one, two))]
    for copy in copies:
        copy.start()
    order = channel_order()
    for layer, copy in enumerate(copies):
        copy.wait()
        parts = [near[layer, t].astype(F32) for t in range(27)] + [jnp.zeros((4, 128), F32)]
        taps = jnp.concatenate(parts, 0).astype(BF16)
        taps = jnp.dot(taps, order, preferred_element_type=F32).astype(BF16)
        for zl in range(4):
            out[zl, layer * 7 : layer * 7 + 7] = taps.reshape(7, 16, 128)


def pack_rows(volume, cotangent, out, near, sems):
    for source, start, halo, count in ((volume, 0, 3, ROWS), (cotangent, ROWS, 1, COTS)):
        planes = [source[ch, z].astype(F32) for z in range(4) for ch in range(4)]
        rows = jnp.swapaxes(jnp.stack(planes), 0, 1).astype(BF16)
        for chip in range(16):
            for r in range(count):
                row = 2 * chip + r - halo
                if 0 <= row < 32:
                    near[chip, start + r] = rows[row]
                else:
                    near[chip, start + r] = jnp.zeros((16, 128), BF16)
    copies = [pltpu.make_async_copy(near.at[chip], out.at[chip], sems.at[chip]) for chip in range(16)]
    for copy in copies:
        copy.start()
    for copy in copies:
        copy.wait()


def hold(packed, after, out):
    pass


def sum_ring(parts, after, out):
    total = parts[0].astype(F32)
    for n in range(1, 16):
        total = total + parts[n].astype(F32)
    total = total.reshape(7, 2, 2, 8, 128)
    for h in range(2):
        for p, piece in enumerate(merge(total[:, 0, h], total[:, 1, h])):
            piece = piece.reshape(56, 128).astype(BF16)
            for zh in range(4):
                out[zh * 4 + 2 * h + p] = piece


def sum_pieces(pieces, total):
    found = pieces[...].astype(F32).sum(0).astype(BF16)
    found = lax.dot_general(
        found, channel_order(), (((1,), (1,)), ((), ())), preferred_element_type=F32
    ).astype(BF16)
    for y in range(4):
        total[y] = found


def pick_line(place, line, after, out):
    for zl in range(4):
        out[zl] = line[zl, place[1] // 4]


def pick_ring(place, ring, out):
    for x in range(4):
        for zl in range(4):
            out[x, zl] = ring[x, zl, place[1] % 4, 1 - place[0]]


def join_rows(place, ring, other, out, near, sent):
    core, tiles = place[0], []
    for zl in range(4):
        for x in range(4):
            mine = ring[x, zl, place[1] % 4, core].astype(F32)
            came = other[x, zl].astype(F32)
            tiles += [jnp.where(core == 0, mine, came), jnp.where(core == 0, came, mine)]
    rows = jnp.swapaxes(jnp.stack(tiles), 0, 1).astype(BF16)
    for z in range(4):
        for ch in range(4):
            near[ch, z] = rows[z * 4 + ch]
    copy = pltpu.make_async_copy(near, out, sent)
    copy.start()
    copy.wait()


VMEM = pl.BlockSpec(memory_space=pltpu.VMEM)
HBM = pl.BlockSpec(memory_space=pltpu.HBM)


def on_chip(kernel, shapes, specs, *arrays, out_specs=VMEM, room=24, **options):
    return pl.pallas_call(
        kernel,
        out_shape=shapes,
        in_specs=specs,
        out_specs=out_specs,
        compiler_params=pltpu.CompilerParams(vmem_limit_bytes=room * 1024 * 1024),
        **options,
    )(*arrays)


def own_taps(weight):
    return jnp.transpose(weight.reshape(27, 128, 4), (0, 2, 1))


def exchange(array, axis):
    return lax.all_to_all(array, axis, split_axis=0, concat_axis=0, tiled=True)


def on_device(activations, weight_one, weight_two, grad_out):
    core = lax.axis_index("c")
    chip = lax.axis_index(CHIPS)
    taps = on_chip(
        pack_taps, jax.ShapeDtypeStruct((4, 14, 16, 128), BF16), [HBM, HBM],
        own_taps(weight_one), own_taps(weight_two),
        scratch_shapes=[pltpu.VMEM((2, 27, 4, 128), BF16), pltpu.SemaphoreType.DMA((2,))],
        room=60, name="pack_taps",
    )
    line = exchange(taps, "zl")
    packed = on_chip(
        pack_rows, jax.ShapeDtypeStruct((16, ROWS + COTS, 16, 128), BF16), [VMEM, VMEM],
        activations[0], grad_out[0], out_specs=HBM, scratch_shapes=[
            pltpu.VMEM((16, ROWS + COTS, 16, 128), BF16), pltpu.SemaphoreType.DMA((16,)),
        ],
        name="pack_rows",
    )
    packed = on_chip(
        hold, jax.ShapeDtypeStruct(packed.shape, BF16), [HBM, HBM], packed, line,
        out_specs=HBM, input_output_aliases={0: 0}, name="hold",
    )
    mine = exchange(packed, CHIPS)
    mine_taps = lax.all_gather(line[None], "x", axis=0, tiled=True)
    swap = [(0, 1), (1, 0)]
    other, other_taps = lax.ppermute(mine, "c", swap), lax.ppermute(mine_taps, "c", swap)
    place = jnp.stack([core, chip]).astype(jnp.int32)
    tiles, grads = compute(place, mine, other, mine_taps, other_taps)

    parts = exchange(grads.reshape(16, 14, 16, 128), ("x", "y"))
    out_line = lax.all_gather(tiles.reshape(1, 4, 4, 2, 16, 128), "zl", axis=0, tiled=True)
    spread = on_chip(
        sum_ring, jax.ShapeDtypeStruct((16, 56, 128), BF16), [VMEM, HBM], parts, out_line, name="sum_ring"
    )
    depth = exchange(spread, ("zh", "zl"))
    piece = on_chip(sum_pieces, jax.ShapeDtypeStruct((4, 56, 128), BF16), [VMEM], depth, name="sum_pieces")
    every = exchange(piece, "y")
    found = jnp.transpose(every.reshape(4, 2, 7, 4, 128), (1, 0, 2, 3, 4)).reshape(2, 28, 4, 128)
    found = jnp.transpose(found[:, :27].astype(F32), (0, 1, 3, 2)).reshape(2, 3, 3, 3, 128, 4)

    smem = pl.BlockSpec(memory_space=pltpu.SMEM)
    out_line = on_chip(
        pick_line, jax.ShapeDtypeStruct((4, 4, 2, 16, 128), BF16), [smem, VMEM, HBM],
        place, out_line, spread, name="pick_line",
    )
    out_ring = lax.all_gather(out_line[None], "x", axis=0, tiled=True)
    sent = on_chip(
        pick_ring, jax.ShapeDtypeStruct((4, 4, 16, 128), BF16), [smem, VMEM], place, out_ring, name="pick_ring"
    )
    result = on_chip(
        join_rows, jax.ShapeDtypeStruct((4, 4, 32, 128), BF16), [smem, VMEM, VMEM],
        place, out_ring, lax.ppermute(sent, "c", swap),
        out_specs=HBM,
        scratch_shapes=[pltpu.VMEM((4, 4, 32, 128), BF16), pltpu.SemaphoreType.DMA],
        name="join_rows",
    )
    return (result[None], found[0], found[1])


def solution(mesh):
    fine = Mesh(np.asarray(mesh.devices).reshape(4, 4, 2, 4, 4), ("zl", "x", "c", "zh", "y"))
    volumes = P(DP, FILT, None, None, None)
    filters = P(None, None, None, None, FILT)
    return jax.shard_map(
        on_device,
        mesh=fine,
        in_specs=(volumes, filters, filters, volumes),
        out_specs=(volumes, filters, filters),
        check_vma=False,
    )
```

```python
import jax
import jax.numpy as jnp
import numpy as np
from jax import lax
from jax.experimental import pallas as pl
from jax.experimental.pallas import tpu as pltpu
from jax.sharding import Mesh, PartitionSpec as P

SLOPE = 0.3
CHIPS = ("zl", "x")
FILT = ("zl", "x", "c")
DP = ("zh", "y")
F32 = jnp.float32
BF16 = jnp.bfloat16
ROWS, COTS, TAPS = 8, 4, 28


def low_half(shape):
    return lax.broadcasted_iota(jnp.int32, shape, len(shape) - 2) < 4


def swap_halves(tiles):
    return pltpu.roll(tiles, 4, tiles.ndim - 2)


def channel_order():
    row = lax.broadcasted_iota(jnp.int32, (128, 128), 0)
    column = lax.broadcasted_iota(jnp.int32, (128, 128), 1)
    core, x, zl, last = column // 64, column // 16 % 4, column // 4 % 4, column % 4
    return jnp.where(row == 32 * zl + 8 * x + 4 * core + last, 1.0, 0.0).astype(BF16)


def merge(even, odd):
    low = low_half(even.shape)
    return jnp.where(low, even, swap_halves(odd)), jnp.where(low, swap_halves(even), odd)


def shift_lanes(block, by):
    lane = lax.broadcasted_iota(jnp.int32, block.shape, 1)
    edge = 0 if by > 0 else 127
    return jnp.where(lane == edge, 0.0, pltpu.roll(block, by % 128, 1))


def conv_plane(weights, source, depth, rows, first_row):
    low, high = max(depth - 1, 0), min(depth + 1, 3)
    taps = slice((low - depth + 1) * 128, (high - depth + 2) * 128)
    total = jnp.dot(
        jnp.concatenate([weights[b, :, taps] for b in range(3)], 1),
        jnp.concatenate([
            source[low * 128 : (high + 1) * 128, (first_row + b) * 128 : (first_row + b + rows) * 128]
            for b in range(3)
        ], 0),
        preferred_element_type=F32,
    )
    out = []
    for r in range(rows):
        block = total[:, r * 128 : (r + 1) * 128]
        out.append(
            block[128:256] + shift_lanes(block[:128], 1) + shift_lanes(block[256:], -1)
        )
    return out


def put_errors(shifted, block, core, depth, row):
    own = jnp.where(core == 0, block[:64], block[64:])
    lanes = slice((depth * 2 + row) * 128, (depth * 2 + row + 1) * 128)
    shifted[0:64, lanes] = shift_lanes(own, -1).astype(BF16)
    shifted[64:128, lanes] = own.astype(BF16)
    shifted[128:192, lanes] = shift_lanes(own, 1).astype(BF16)


def tap_grad(shifted, source, first_row, total, out, which):
    for b in range(3):
        lanes = slice((first_row + b) * 128, (first_row + b + 2) * 128)
        total[...] = jnp.zeros_like(total)
        for depth in range(4):
            low, high = max(depth - 1, 0), min(depth + 1, 3)
            taps = slice((low - depth + 1) * 128, (high - depth + 2) * 128)
            total[:, taps] += lax.dot_general(
                shifted[:, depth * 256 : (depth + 1) * 256],
                source[low * 128 : (high + 1) * 128, lanes],
                (((1,), (1,)), ((), ())),
                preferred_element_type=F32,
            )
        for a in range(3):
            for e in range(3):
                tap = a * 9 + b * 3 + e
                for x in range(4):
                    out[x, tap // 7, which * 7 + tap % 7] = total[
                        e * 64 + x * 16 : e * 64 + (x + 1) * 16, a * 128 : (a + 1) * 128
                    ].astype(BF16)


def planes(group, h):
    halves = [[tile.astype(F32)[h * 8 : h * 8 + 8] for tile in line] for line in group]
    even = jnp.stack([line[zl] for line in halves for zl in (0, 2)])
    odd = jnp.stack([line[zl] for line in halves for zl in (1, 3)])
    return [plane.reshape(64, 128).astype(BF16) for plane in merge(even, odd)]


def place_half(side, rows, taps, act, cot, w_one, w_two):
    def rows_of(first):
        return pl.ds(pl.multiple_of(first + 64 * side, 64), 64)

    for layer, into in enumerate((w_one, w_two)):
        for step in range(7):
            group = [[taps[x, zl, layer * 7 + step] for zl in range(4)] for x in range(4)]
            for h in range(2):
                for p, plane in enumerate(planes(group, h)):
                    tap = 4 * step + 2 * h + p
                    if tap < 27:
                        a, b, e = tap // 9, tap // 3 % 3, tap % 3
                        into[b, rows_of(e * 128), a * 128 : (a + 1) * 128] = plane
    for first, count, into in ((0, ROWS, act), (ROWS, COTS, cot)):
        for r in range(count):
            group = [[rows[zl * 4 + x, first + r] for zl in range(4)] for x in range(4)]
            for h in range(2):
                for p, plane in enumerate(planes(group, h)):
                    into[rows_of((2 * h + p) * 128), r * 128 : (r + 1) * 128] = plane


def place_mine(place, mine, taps, act, cot, w_one, w_two):
    place_half(place[0], mine, taps, act, cot, w_one, w_two)


def work(
    place, far, other_taps, act_in, cot_in, one_in, two_in,
    out_tiles, grads, act, cot, w_one, w_two,
    hid, err, w_back, pre, shifted, total, near, sems,
):
    core, chip = place[0], place[1]
    place_half(1 - core, far, other_taps, act, cot, w_one, w_two)
    for a in range(3):
        for b in range(3):
            for e in range(3):
                block = w_two[b, e * 128 : (e + 1) * 128, a * 128 : (a + 1) * 128]
                w_back[2 - b, (2 - e) * 128 : (3 - e) * 128, (2 - a) * 128 : (3 - a) * 128] = block.T

    for z in range(4):
        for r, value in enumerate(conv_plane(w_one, act, z, 6, 0)):
            row = 2 * chip - 2 + r
            inside = jnp.logical_and(row >= 0, row < 32)
            if r in (2, 3):
                pre[z * 128 : (z + 1) * 128, (r - 2) * 128 : (r - 1) * 128] = value
            kept = jnp.where(inside, jnp.where(value > 0, value, SLOPE * value), 0.0)
            hid[z * 128 : (z + 1) * 128, r * 128 : (r + 1) * 128] = kept.astype(BF16)

    held = {}
    for z in range(4):
        values = conv_plane(w_two, hid, z, 4, 0)
        for r, value in enumerate(values):
            at = (slice(z * 128, (z + 1) * 128), slice(r * 128, (r + 1) * 128))
            error = cot[at].astype(F32) * jnp.where(value > 0, 1.0, SLOPE)
            err[at] = error.astype(BF16)
            if r in (1, 2):
                put_errors(shifted, error, core, z, r - 1)
        for r in range(2):
            own = jnp.where(core == 0, values[1 + r][:64], values[1 + r][64:])
            held[z % 2, r] = jnp.where(own > 0, own, SLOPE * own).reshape(4, 2, 8, 128)
            if z % 2:
                half = slice((z // 2) * 8, (z // 2) * 8 + 8)
                for odd, tile in enumerate(merge(held[0, r], held[1, r])):
                    for x in range(4):
                        for pair in range(2):
                            out_tiles[(2 * pair + odd) * 4 + x, r, half] = tile[x, pair].astype(BF16)

    for x in range(4):
        for g in range(2):
            near[x, 3, g * 7 + 6] = jnp.zeros((16, 128), BF16)
    tap_grad(shifted, hid, 1, total, near, 1)
    second = pltpu.make_async_copy(near.at[:, :, 7:14], grads.at[:, :, 7:14], sems.at[1])
    second.start()

    for z in range(4):
        for r, value in enumerate(conv_plane(w_back, err, z, 2, 0)):
            slope = jnp.where(
                pre[z * 128 : (z + 1) * 128, r * 128 : (r + 1) * 128] > 0, 1.0, SLOPE
            )
            put_errors(shifted, value * slope, core, z, r)
    tap_grad(shifted, act, 2, total, near, 0)
    first = pltpu.make_async_copy(near.at[:, :, 0:7], grads.at[:, :, 0:7], sems.at[0])
    first.start()
    second.wait()
    first.wait()


def compute(place, mine, far, mine_taps, other_taps):
    smem = pl.BlockSpec(memory_space=pltpu.SMEM)
    halves = (
        jax.ShapeDtypeStruct((512, ROWS * 128), BF16),
        jax.ShapeDtypeStruct((512, COTS * 128), BF16),
        jax.ShapeDtypeStruct((3, 384, 384), BF16),
        jax.ShapeDtypeStruct((3, 384, 384), BF16),
    )
    half = on_chip(
        place_mine, halves, [smem, VMEM, VMEM], place, mine, mine_taps, out_specs=(VMEM,) * 4, name="place_mine"
    )
    tiles, grads, *_ = on_chip(
        work,
        (
            jax.ShapeDtypeStruct((16, 2, 16, 128), BF16),
            jax.ShapeDtypeStruct((4, 4, 14, 16, 128), BF16),
            *halves,
        ),
        [smem] + [VMEM] * 6, place, far, other_taps, *half,
        out_specs=(VMEM, HBM) + (VMEM,) * 4,
        input_output_aliases={3: 2, 4: 3, 5: 4, 6: 5},
        scratch_shapes=[
            pltpu.VMEM((512, 768), BF16),
            pltpu.VMEM((512, 512), BF16),
            pltpu.VMEM((3, 384, 384), BF16),
            pltpu.VMEM((512, 256), F32),
            pltpu.VMEM((192, 1024), BF16),
            pltpu.VMEM((192, 384), F32),
            pltpu.VMEM((4, 4, 14, 16, 128), BF16),
            pltpu.SemaphoreType.DMA((2,)),
        ],
        cost_estimate=pl.CostEstimate(flops=6_300_000_000, bytes_accessed=6_000_000, transcendentals=0),
        name="convolutions",
    )
    return tiles, grads


def pack_taps(one, two, out, near, sems):
    copies = [pltpu.make_async_copy(taps, near.at[n], sems.at[n]) for n, taps in enumerate((one, two))]
    for copy in copies:
        copy.start()
    order = channel_order()
    for layer, copy in enumerate(copies):
        copy.wait()
        parts = [near[layer, t].astype(F32) for t in range(27)] + [jnp.zeros((4, 128), F32)]
        taps = jnp.concatenate(parts, 0).astype(BF16)
        taps = jnp.dot(taps, order, preferred_element_type=F32).astype(BF16)
        for zl in range(4):
            out[zl, layer * 7 : layer * 7 + 7] = taps.reshape(7, 16, 128)


def pack_rows(volume, cotangent, out, near, sems):
    for source, start, halo, count in ((volume, 0, 3, ROWS), (cotangent, ROWS, 1, COTS)):
        planes = [source[ch, z].astype(F32) for z in range(4) for ch in range(4)]
        rows = jnp.swapaxes(jnp.stack(planes), 0, 1).astype(BF16)
        for chip in range(16):
            for r in range(count):
                row = 2 * chip + r - halo
                if 0 <= row < 32:
                    near[chip, start + r] = rows[row]
                else:
                    near[chip, start + r] = jnp.zeros((16, 128), BF16)
    copies = [pltpu.make_async_copy(near.at[chip], out.at[chip], sems.at[chip]) for chip in range(16)]
    for copy in copies:
        copy.start()
    for copy in copies:
        copy.wait()


def hold(packed, after, out):
    pass


def sum_ring(parts, after, out):
    total = parts[0].astype(F32)
    for n in range(1, 16):
        total = total + parts[n].astype(F32)
    total = total.reshape(7, 2, 2, 8, 128)
    for h in range(2):
        for p, piece in enumerate(merge(total[:, 0, h], total[:, 1, h])):
            piece = piece.reshape(56, 128).astype(BF16)
            for zh in range(4):
                out[zh * 4 + 2 * h + p] = piece


def sum_pieces(pieces, after, total):
    found = pieces[...].astype(F32).sum(0).astype(BF16)
    found = lax.dot_general(
        found, channel_order(), (((1,), (1,)), ((), ())), preferred_element_type=F32
    ).astype(BF16)
    for y in range(4):
        total[y] = found


def pick_line(place, line, after, out):
    for zl in range(4):
        out[zl] = line[zl, place[1] // 4]


def join_rows(place, ring, after, out, near, sent):
    tiles = []
    for zl in range(4):
        for x in range(4):
            for r in range(2):
                tiles.append(ring[x, zl, place[1] % 4, r].astype(F32))
    rows = jnp.swapaxes(jnp.stack(tiles), 0, 1).astype(BF16)
    for z in range(4):
        for ch in range(4):
            near[ch, z] = rows[z * 4 + ch]
    copy = pltpu.make_async_copy(near, out, sent)
    copy.start()
    copy.wait()


VMEM = pl.BlockSpec(memory_space=pltpu.VMEM)
HBM = pl.BlockSpec(memory_space=pltpu.HBM)


def on_chip(kernel, shapes, specs, *arrays, out_specs=VMEM, room=24, **options):
    return pl.pallas_call(
        kernel,
        out_shape=shapes,
        in_specs=specs,
        out_specs=out_specs,
        compiler_params=pltpu.CompilerParams(vmem_limit_bytes=room * 1024 * 1024),
        **options,
    )(*arrays)


def own_taps(weight):
    return jnp.transpose(weight.reshape(27, 128, 4), (0, 2, 1))


def exchange(array, axis):
    return lax.all_to_all(array, axis, split_axis=0, concat_axis=0, tiled=True)


def on_device(activations, weight_one, weight_two, grad_out):
    core = lax.axis_index("c")
    chip = lax.axis_index(CHIPS)
    taps = on_chip(
        pack_taps, jax.ShapeDtypeStruct((4, 14, 16, 128), BF16), [HBM, HBM],
        own_taps(weight_one), own_taps(weight_two),
        scratch_shapes=[pltpu.VMEM((2, 27, 4, 128), BF16), pltpu.SemaphoreType.DMA((2,))],
        room=60, name="pack_taps",
    )
    line = exchange(taps, "zl")
    packed = on_chip(
        pack_rows, jax.ShapeDtypeStruct((16, ROWS + COTS, 16, 128), BF16), [VMEM, VMEM],
        activations[0], grad_out[0], out_specs=HBM, scratch_shapes=[
            pltpu.VMEM((16, ROWS + COTS, 16, 128), BF16), pltpu.SemaphoreType.DMA((16,)),
        ],
        name="pack_rows",
    )
    packed = on_chip(
        hold, jax.ShapeDtypeStruct(packed.shape, BF16), [HBM, HBM], packed, line,
        out_specs=HBM, input_output_aliases={0: 0}, name="hold",
    )
    mine = exchange(packed, CHIPS)
    mine_taps = lax.all_gather(line[None], "x", axis=0, tiled=True)
    swap = [(0, 1), (1, 0)]
    other, other_taps = lax.ppermute(mine, "c", swap), lax.ppermute(mine_taps, "c", swap)
    place = jnp.stack([core, chip]).astype(jnp.int32)
    tiles, grads = compute(place, mine, other, mine_taps, other_taps)

    parts = exchange(grads.reshape(16, 14, 16, 128), ("x", "y"))
    out_line = lax.all_gather(tiles.reshape(1, 4, 4, 2, 16, 128), "zl", axis=0, tiled=True)
    spread = on_chip(
        sum_ring, jax.ShapeDtypeStruct((16, 56, 128), BF16), [VMEM, HBM], parts, out_line, name="sum_ring"
    )
    depth = exchange(spread, ("zh", "zl"))
    smem = pl.BlockSpec(memory_space=pltpu.SMEM)
    out_line = on_chip(
        pick_line, jax.ShapeDtypeStruct((4, 4, 2, 16, 128), BF16), [smem, VMEM, HBM],
        place, out_line, spread, name="pick_line",
    )
    out_ring = lax.all_gather(out_line[None], "x", axis=0, tiled=True)
    piece = on_chip(
        sum_pieces, jax.ShapeDtypeStruct((4, 56, 128), BF16), [VMEM, HBM], depth, out_ring, name="sum_pieces"
    )
    every = exchange(piece, "y")
    found = jnp.transpose(every.reshape(4, 2, 7, 4, 128), (1, 0, 2, 3, 4)).reshape(2, 28, 4, 128)
    found = jnp.transpose(found[:, :27].astype(F32), (0, 1, 3, 2)).reshape(2, 3, 3, 3, 128, 4)

    result = on_chip(
        join_rows, jax.ShapeDtypeStruct((4, 4, 32, 128), BF16), [smem, VMEM, HBM], place, out_ring, piece,
        out_specs=HBM,
        scratch_shapes=[pltpu.VMEM((4, 4, 32, 128), BF16), pltpu.SemaphoreType.DMA],
        name="join_rows",
    )
    return (result[None], found[0], found[1])


def solution(mesh):
    fine = Mesh(np.asarray(mesh.devices).reshape(4, 4, 2, 4, 4), ("zl", "x", "c", "zh", "y"))
    volumes = P(DP, FILT, None, None, None)
    filters = P(None, None, None, None, FILT)
    return jax.shard_map(
        on_device,
        mesh=fine,
        in_specs=(volumes, filters, filters, volumes),
        out_specs=(volumes, filters, filters),
        check_vma=False,
    )
```

```python
import jax
import jax.numpy as jnp
import numpy as np
from jax import lax
from jax.experimental import pallas as pl
from jax.experimental.pallas import tpu as pltpu
from jax.sharding import Mesh, PartitionSpec as P

SLOPE = 0.3
CHIPS = ("zl", "x")
FILT = ("zl", "x", "c")
DP = ("zh", "y")
F32 = jnp.float32
BF16 = jnp.bfloat16
ROWS, COTS, TAPS = 8, 4, 28


def low_half(shape):
    return lax.broadcasted_iota(jnp.int32, shape, len(shape) - 2) < 4


def swap_halves(tiles):
    return pltpu.roll(tiles, 4, tiles.ndim - 2)


def channel_order():
    row = lax.broadcasted_iota(jnp.int32, (128, 128), 0)
    column = lax.broadcasted_iota(jnp.int32, (128, 128), 1)
    core, x, zl, last = column // 64, column // 16 % 4, column // 4 % 4, column % 4
    return jnp.where(row == 32 * zl + 8 * x + 4 * core + last, 1.0, 0.0).astype(BF16)


def merge(even, odd):
    low = low_half(even.shape)
    return jnp.where(low, even, swap_halves(odd)), jnp.where(low, swap_halves(even), odd)


def shift_lanes(block, by):
    lane = lax.broadcasted_iota(jnp.int32, block.shape, 1)
    edge = 0 if by > 0 else 127
    return jnp.where(lane == edge, 0.0, pltpu.roll(block, by % 128, 1))


def conv_plane(weights, source, depth, rows, first_row):
    low, high = max(depth - 1, 0), min(depth + 1, 3)
    taps = slice((low - depth + 1) * 128, (high - depth + 2) * 128)
    total = jnp.dot(
        jnp.concatenate([weights[b, :, taps] for b in range(3)], 1),
        jnp.concatenate([
            source[low * 128 : (high + 1) * 128, (first_row + b) * 128 : (first_row + b + rows) * 128]
            for b in range(3)
        ], 0),
        preferred_element_type=F32,
    )
    out = []
    for r in range(rows):
        block = total[:, r * 128 : (r + 1) * 128]
        out.append(
            block[128:256] + shift_lanes(block[:128], 1) + shift_lanes(block[256:], -1)
        )
    return out


def put_errors(shifted, block, core, depth, row):
    own = jnp.where(core == 0, block[:64], block[64:])
    lanes = slice((depth * 2 + row) * 128, (depth * 2 + row + 1) * 128)
    shifted[0:64, lanes] = shift_lanes(own, -1).astype(BF16)
    shifted[64:128, lanes] = own.astype(BF16)
    shifted[128:192, lanes] = shift_lanes(own, 1).astype(BF16)


def tap_grad(shifted, source, first_row, total, out, which):
    for b in range(3):
        lanes = slice((first_row + b) * 128, (first_row + b + 2) * 128)
        total[...] = jnp.zeros_like(total)
        for depth in range(4):
            low, high = max(depth - 1, 0), min(depth + 1, 3)
            taps = slice((low - depth + 1) * 128, (high - depth + 2) * 128)
            total[:, taps] += lax.dot_general(
                shifted[:, depth * 256 : (depth + 1) * 256],
                source[low * 128 : (high + 1) * 128, lanes],
                (((1,), (1,)), ((), ())),
                preferred_element_type=F32,
            )
        for a in range(3):
            for e in range(3):
                tap = a * 9 + b * 3 + e
                for x in range(4):
                    out[x, tap // 7, which * 7 + tap % 7] = total[
                        e * 64 + x * 16 : e * 64 + (x + 1) * 16, a * 128 : (a + 1) * 128
                    ].astype(BF16)


def planes(group, h):
    halves = [[tile.astype(F32)[h * 8 : h * 8 + 8] for tile in line] for line in group]
    even = jnp.stack([line[zl] for line in halves for zl in (0, 2)])
    odd = jnp.stack([line[zl] for line in halves for zl in (1, 3)])
    return [plane.reshape(64, 128).astype(BF16) for plane in merge(even, odd)]


def place_half(side, rows, taps, act, cot, w_one, w_two):
    def rows_of(first):
        return pl.ds(pl.multiple_of(first + 64 * side, 64), 64)

    for layer, into in enumerate((w_one, w_two)):
        for step in range(7):
            group = [[taps[x, zl, layer * 7 + step] for zl in range(4)] for x in range(4)]
            for h in range(2):
                for p, plane in enumerate(planes(group, h)):
                    tap = 4 * step + 2 * h + p
                    if tap < 27:
                        a, b, e = tap // 9, tap // 3 % 3, tap % 3
                        into[b, rows_of(e * 128), a * 128 : (a + 1) * 128] = plane
    for first, count, into in ((0, ROWS, act), (ROWS, COTS, cot)):
        for r in range(count):
            group = [[rows[zl * 4 + x, first + r] for zl in range(4)] for x in range(4)]
            for h in range(2):
                for p, plane in enumerate(planes(group, h)):
                    into[rows_of((2 * h + p) * 128), r * 128 : (r + 1) * 128] = plane


def place_mine(place, mine, taps, act, cot, w_one, w_two):
    place_half(place[0], mine, taps, act, cot, w_one, w_two)


def work(
    place, far, other_taps, act_in, cot_in, one_in, two_in,
    out_tiles, grads, act, cot, w_one, w_two,
    hid, err, w_back, pre, shifted, total, near, sems,
):
    core, chip = place[0], place[1]
    place_half(1 - core, far, other_taps, act, cot, w_one, w_two)
    for a in range(3):
        for b in range(3):
            for e in range(3):
                block = w_two[b, e * 128 : (e + 1) * 128, a * 128 : (a + 1) * 128]
                w_back[2 - b, (2 - e) * 128 : (3 - e) * 128, (2 - a) * 128 : (3 - a) * 128] = block.T

    for z in range(4):
        for r, value in enumerate(conv_plane(w_one, act, z, 6, 0)):
            row = 2 * chip - 2 + r
            inside = jnp.logical_and(row >= 0, row < 32)
            if r in (2, 3):
                pre[z * 128 : (z + 1) * 128, (r - 2) * 128 : (r - 1) * 128] = value
            kept = jnp.where(inside, jnp.where(value > 0, value, SLOPE * value), 0.0)
            hid[z * 128 : (z + 1) * 128, r * 128 : (r + 1) * 128] = kept.astype(BF16)

    held = {}
    for z in range(4):
        values = conv_plane(w_two, hid, z, 4, 0)
        for r, value in enumerate(values):
            at = (slice(z * 128, (z + 1) * 128), slice(r * 128, (r + 1) * 128))
            error = cot[at].astype(F32) * jnp.where(value > 0, 1.0, SLOPE)
            err[at] = error.astype(BF16)
            if r in (1, 2):
                put_errors(shifted, error, core, z, r - 1)
        for r in range(2):
            own = jnp.where(core == 0, values[1 + r][:64], values[1 + r][64:])
            held[z % 2, r] = jnp.where(own > 0, own, SLOPE * own).reshape(4, 2, 8, 128)
            if z % 2:
                half = slice((z // 2) * 8, (z // 2) * 8 + 8)
                for odd, tile in enumerate(merge(held[0, r], held[1, r])):
                    for x in range(4):
                        for pair in range(2):
                            out_tiles[(2 * pair + odd) * 4 + x, r, half] = tile[x, pair].astype(BF16)

    for x in range(4):
        for g in range(2):
            near[x, 3, g * 7 + 6] = jnp.zeros((16, 128), BF16)
    tap_grad(shifted, hid, 1, total, near, 1)
    second = pltpu.make_async_copy(near.at[:, :, 7:14], grads.at[:, :, 7:14], sems.at[1])
    second.start()

    for z in range(4):
        for r, value in enumerate(conv_plane(w_back, err, z, 2, 0)):
            slope = jnp.where(
                pre[z * 128 : (z + 1) * 128, r * 128 : (r + 1) * 128] > 0, 1.0, SLOPE
            )
            put_errors(shifted, value * slope, core, z, r)
    tap_grad(shifted, act, 2, total, near, 0)
    first = pltpu.make_async_copy(near.at[:, :, 0:7], grads.at[:, :, 0:7], sems.at[0])
    first.start()
    second.wait()
    first.wait()


def compute(place, mine, far, mine_taps, other_taps):
    smem = pl.BlockSpec(memory_space=pltpu.SMEM)
    halves = (
        jax.ShapeDtypeStruct((512, ROWS * 128), BF16),
        jax.ShapeDtypeStruct((512, COTS * 128), BF16),
        jax.ShapeDtypeStruct((3, 384, 384), BF16),
        jax.ShapeDtypeStruct((3, 384, 384), BF16),
    )
    half = on_chip(
        place_mine, halves, [smem, VMEM, VMEM], place, mine, mine_taps, out_specs=(VMEM,) * 4, name="place_mine"
    )
    tiles, grads, *_ = on_chip(
        work,
        (
            jax.ShapeDtypeStruct((16, 2, 16, 128), BF16),
            jax.ShapeDtypeStruct((4, 4, 14, 16, 128), BF16),
            *halves,
        ),
        [smem] + [VMEM] * 6, place, far, other_taps, *half,
        out_specs=(VMEM, HBM) + (VMEM,) * 4,
        input_output_aliases={3: 2, 4: 3, 5: 4, 6: 5},
        scratch_shapes=[
            pltpu.VMEM((512, 768), BF16),
            pltpu.VMEM((512, 512), BF16),
            pltpu.VMEM((3, 384, 384), BF16),
            pltpu.VMEM((512, 256), F32),
            pltpu.VMEM((192, 1024), BF16),
            pltpu.VMEM((192, 384), F32),
            pltpu.VMEM((4, 4, 14, 16, 128), BF16),
            pltpu.SemaphoreType.DMA((2,)),
        ],
        cost_estimate=pl.CostEstimate(flops=6_300_000_000, bytes_accessed=6_000_000, transcendentals=0),
        name="convolutions",
    )
    return tiles, grads


def pack_taps(one, two, out, near, sems):
    copies = [pltpu.make_async_copy(taps, near.at[n], sems.at[n]) for n, taps in enumerate((one, two))]
    for copy in copies:
        copy.start()
    order = channel_order()
    for layer, copy in enumerate(copies):
        copy.wait()
        parts = [near[layer, t].astype(F32) for t in range(27)] + [jnp.zeros((4, 128), F32)]
        taps = jnp.concatenate(parts, 0).astype(BF16)
        taps = jnp.dot(taps, order, preferred_element_type=F32).astype(BF16)
        for zl in range(4):
            out[zl, layer * 7 : layer * 7 + 7] = taps.reshape(7, 16, 128)


def pack_rows(volume, cotangent, out, near, sems):
    for source, start, halo, count in ((volume, 0, 3, ROWS), (cotangent, ROWS, 1, COTS)):
        planes = [source[ch, z].astype(F32) for z in range(4) for ch in range(4)]
        rows = jnp.swapaxes(jnp.stack(planes), 0, 1).astype(BF16)
        for chip in range(16):
            for r in range(count):
                row = 2 * chip + r - halo
                if 0 <= row < 32:
                    near[chip, start + r] = rows[row]
                else:
                    near[chip, start + r] = jnp.zeros((16, 128), BF16)
    copies = [pltpu.make_async_copy(near.at[chip], out.at[chip], sems.at[chip]) for chip in range(16)]
    for copy in copies:
        copy.start()
    for copy in copies:
        copy.wait()


def hold(packed, after, out):
    pass


def sum_ring(parts, one, two, three, out):
    total = parts[0].astype(F32)
    for n in range(1, 16):
        total = total + parts[n].astype(F32)
    total = total.reshape(7, 2, 2, 8, 128)
    for h in range(2):
        for p, piece in enumerate(merge(total[:, 0, h], total[:, 1, h])):
            piece = piece.reshape(56, 128).astype(BF16)
            for zh in range(4):
                out[zh * 4 + 2 * h + p] = piece


def sum_pieces(pieces, after, total):
    found = pieces[...].astype(F32).sum(0).astype(BF16)
    found = lax.dot_general(
        found, channel_order(), (((1,), (1,)), ((), ())), preferred_element_type=F32
    ).astype(BF16)
    for y in range(4):
        total[y] = found


def pick_line(place, tiles, *outs):
    for m, out in enumerate(outs):
        out[...] = tiles[pl.ds((place[1] // 4 ^ m) * 4, 4)]


def join_line(own, one, two, three, after, out):
    for m, tiles in enumerate((own, one, two, three)):
        out[m] = tiles[...]


def join_rows(place, ring, after, out, near, sent):
    tiles = []
    for zl in range(4):
        for x in range(4):
            for r in range(2):
                tiles.append(ring[x, zl ^ (place[1] // 4), place[1] % 4, r].astype(F32))
    rows = jnp.swapaxes(jnp.stack(tiles), 0, 1).astype(BF16)
    for z in range(4):
        for ch in range(4):
            near[ch, z] = rows[z * 4 + ch]
    copy = pltpu.make_async_copy(near, out, sent)
    copy.start()
    copy.wait()


VMEM = pl.BlockSpec(memory_space=pltpu.VMEM)
HBM = pl.BlockSpec(memory_space=pltpu.HBM)


def on_chip(kernel, shapes, specs, *arrays, out_specs=VMEM, room=24, **options):
    return pl.pallas_call(
        kernel,
        out_shape=shapes,
        in_specs=specs,
        out_specs=out_specs,
        compiler_params=pltpu.CompilerParams(vmem_limit_bytes=room * 1024 * 1024),
        **options,
    )(*arrays)


def own_taps(weight):
    return jnp.transpose(weight.reshape(27, 128, 4), (0, 2, 1))


def exchange(array, axis):
    return lax.all_to_all(array, axis, split_axis=0, concat_axis=0, tiled=True)


def on_device(activations, weight_one, weight_two, grad_out):
    core = lax.axis_index("c")
    chip = lax.axis_index(CHIPS)
    taps = on_chip(
        pack_taps, jax.ShapeDtypeStruct((4, 14, 16, 128), BF16), [HBM, HBM],
        own_taps(weight_one), own_taps(weight_two),
        scratch_shapes=[pltpu.VMEM((2, 27, 4, 128), BF16), pltpu.SemaphoreType.DMA((2,))],
        room=60, name="pack_taps",
    )
    line = exchange(taps, "zl")
    packed = on_chip(
        pack_rows, jax.ShapeDtypeStruct((16, ROWS + COTS, 16, 128), BF16), [VMEM, VMEM],
        activations[0], grad_out[0], out_specs=HBM, scratch_shapes=[
            pltpu.VMEM((16, ROWS + COTS, 16, 128), BF16), pltpu.SemaphoreType.DMA((16,)),
        ],
        name="pack_rows",
    )
    packed = on_chip(
        hold, jax.ShapeDtypeStruct(packed.shape, BF16), [HBM, HBM], packed, line,
        out_specs=HBM, input_output_aliases={0: 0}, name="hold",
    )
    mine = exchange(packed, CHIPS)
    mine_taps = lax.all_gather(line[None], "x", axis=0, tiled=True)
    swap = [(0, 1), (1, 0)]
    other, other_taps = lax.ppermute(mine, "c", swap), lax.ppermute(mine_taps, "c", swap)
    place = jnp.stack([core, chip]).astype(jnp.int32)
    tiles, grads = compute(place, mine, other, mine_taps, other_taps)

    parts = exchange(grads.reshape(16, 14, 16, 128), ("x", "y"))
    smem = pl.BlockSpec(memory_space=pltpu.SMEM)
    tile = jax.ShapeDtypeStruct((4, 2, 16, 128), BF16)
    own, *sent = on_chip(pick_line, (tile,) * 4, [smem, VMEM], place, tiles, out_specs=(VMEM,) * 4, name="pick_line")
    came = [
        lax.ppermute(part, "zl", [(i, i ^ m) for i in range(4)]) for m, part in zip((1, 2, 3), sent)
    ]
    spread = on_chip(
        sum_ring, jax.ShapeDtypeStruct((16, 56, 128), BF16), [VMEM, HBM, HBM, HBM], parts, *came, name="sum_ring"
    )
    depth = exchange(spread, ("zh", "zl"))
    out_line = on_chip(
        join_line, jax.ShapeDtypeStruct((4, 4, 2, 16, 128), BF16), [VMEM] * 4 + [HBM],
        own, *came, spread, name="join_line",
    )
    out_ring = lax.all_gather(out_line[None], "x", axis=0, tiled=True)
    piece = on_chip(
        sum_pieces, jax.ShapeDtypeStruct((4, 56, 128), BF16), [VMEM, HBM], depth, out_ring, name="sum_pieces"
    )
    every = exchange(piece, "y")
    found = jnp.transpose(every.reshape(4, 2, 7, 4, 128), (1, 0, 2, 3, 4)).reshape(2, 28, 4, 128)
    found = jnp.transpose(found[:, :27].astype(F32), (0, 1, 3, 2)).reshape(2, 3, 3, 3, 128, 4)

    result = on_chip(
        join_rows, jax.ShapeDtypeStruct((4, 4, 32, 128), BF16), [smem, VMEM, HBM], place, out_ring, piece,
        out_specs=HBM,
        scratch_shapes=[pltpu.VMEM((4, 4, 32, 128), BF16), pltpu.SemaphoreType.DMA],
        name="join_rows",
    )
    return (result[None], found[0], found[1])


def solution(mesh):
    fine = Mesh(np.asarray(mesh.devices).reshape(4, 4, 2, 4, 4), ("zl", "x", "c", "zh", "y"))
    volumes = P(DP, FILT, None, None, None)
    filters = P(None, None, None, None, FILT)
    return jax.shard_map(
        on_device,
        mesh=fine,
        in_specs=(volumes, filters, filters, volumes),
        out_specs=(volumes, filters, filters),
        check_vma=False,
    )
```
